256 devices in a mesh: rep: 4 (over y_hi, core), fsdp: 64 (over z, y_lo, x).
Axes of the slice: x: 4, y: 4 (y_hi: 2, y_lo: 2; y = y_hi * 2 + y_lo), z: 8, core: 2. Of those that a mesh axis runs over, the one named last changes fastest.
Arguments:
- tokens_in: bfloat16 [4096, 4096], P(('rep', 'fsdp')), may hold values from -6 to 6
- cotangent: bfloat16 [4096, 4096], P(('rep', 'fsdp')), may hold values from -12 to 12
- gate_weight: bfloat16 [4, 7168, 4096], P('rep', 'fsdp'), may hold values from -6 to 6
- up_master: float32 [4, 7168, 4096], P('rep', 'fsdp'), may hold values from -6 to 6
- down_weight: bfloat16 [4, 7168, 4096], P('rep', 'fsdp'), may hold values from -6 to 6
- up_first: bfloat16 [4, 7168, 4096], P('rep', 'fsdp'), may hold values from -4 to 4
- up_second: bfloat16 [4, 7168, 4096], P('rep', 'fsdp'), may hold values from 0.019897461 to 1
- snapshot: bfloat16 [4, 4096, 4096], P('rep', 'fsdp'), may hold values from -6 to 6
- global_params: float32 [4096, 4096], P('fsdp', 'rep'), may hold values from -6 to 6
- outer_momentum: float32 [4096, 4096], P('fsdp', 'rep'), may hold values from -4 to 4
Outputs:
- input_grad: bfloat16 [4096, 4096], P(('rep', 'fsdp'))
- up_new: float32 [4, 7168, 4096], P('rep', 'fsdp')
- first_new: bfloat16 [4, 7168, 4096], P('rep', 'fsdp')
- second_new: bfloat16 [4, 7168, 4096], P('rep', 'fsdp')
- global_new: float32 [4096, 4096], P('fsdp', 'rep')
- momentum_new: float32 [4096, 4096], P('fsdp', 'rep')
The draws below stay inside these ranges and needn't reach their ends.
All inputs are finite; a program needn't handle non-finite values.
Results may differ from the reference program's by a relative error of at most 0.009.
Values may be sent and summed in bfloat16 or wider, within the bound.
No kernel may reach another device: no remote copies, remote signals or barrier semaphores. Data moves between devices by JAX's collectives and lax.ppermute only.
A program may use at most 128 MiB of HBM per device.

```python
import math
import jax
import jax.numpy as jnp

D = 4096
FFW = 7168
TOK_REP = 1024
TOKENS = 4096
N_REP = 4


def block_levels(own_key, dims, shards, least, high):
    def one(position, parts):
        draws = jax.random.uniform(jax.random.fold_in(jax.random.fold_in(own_key, 6), position), (parts,), jnp.float32, least / len(shards), high / len(shards))
        return jnp.repeat(jnp.exp(draws), dims[position] // parts).reshape((-1,) + (1,) * (len(dims) - position - 1))

    factor_of = one(*shards[0])
    for cut in shards[1:]:
        factor_of = factor_of * one(*cut)
    return factor_of


def bell_draw(stream_key, extent, spread, bound, split=(), kind=jnp.bfloat16):
    drawn = spread * jax.random.normal(stream_key, extent, jnp.float32)
    if split:
        drawn = drawn * block_levels(stream_key, extent, split, -0.22, 0.18)
    return jnp.clip(drawn, -bound, bound).astype(kind)


def setup_inputs(seed: int = 0) -> dict:
    arg_keys = jax.random.split(jax.random.key(seed), 11)
    return {
        "tokens_in": bell_draw(arg_keys[0], (TOKENS, D), 1.0, 6.0, ((0, 256),)),
        "cotangent": bell_draw(arg_keys[1], (TOKENS, D), 2.0, 12.0, ((0, 256),)),
        "gate_weight": bell_draw(arg_keys[2], (N_REP, FFW, D), 1.0, 6.0, ((0, 4), (1, 64))),
        "up_master": bell_draw(arg_keys[3], (N_REP, FFW, D), 1.0, 6.0, ((0, 4), (1, 64)), jnp.float32),
        "down_weight": bell_draw(arg_keys[4], (N_REP, FFW, D), 1.0, 6.0, ((0, 4), (1, 64))),
        "up_first": bell_draw(arg_keys[5], (N_REP, FFW, D), 0.5, 4.0, ((0, 4), (1, 64))),
        "up_second": jnp.clip(jnp.exp(math.log(1.0) - 3.9171631 * jax.random.uniform(arg_keys[6], (N_REP, FFW, D), jnp.float32) ** block_levels(arg_keys[6], (N_REP, FFW, D), ((0, 4), (1, 64)), -0.2, 0.2)), 0.019897461, 1.0).astype(jnp.bfloat16),
        "snapshot": bell_draw(arg_keys[7], (N_REP, D, D), 1.0, 6.0, ((0, 4), (1, 64))),
        "global_params": bell_draw(arg_keys[8], (D, D), 1.0, 6.0, ((0, 64), (1, 4)), jnp.float32),
        "outer_momentum": bell_draw(arg_keys[9], (D, D), 0.5, 4.0, ((0, 64), (1, 4)), jnp.float32),
    }


beta_one = 0.9
beta_two = 0.95
inner_rate = 0.02
decay_rate = 0.1
adam_eps = 1e-08
bias_one = 0.9999734386011124
bias_two = 0.9940794707796659
outer_rate = 0.7
outer_mu = 0.9

def replica_step(inputs, out_grad, w_gate, w_master, w_down, moment_one, moment_two):
    in_scale = 1.0 / math.sqrt(D)
    hid_scale = 1.0 / math.sqrt(FFW)
    w_up = w_master.astype(jnp.bfloat16)
    pre_gate = jnp.dot(inputs, w_gate.T, preferred_element_type=jnp.float32) * in_scale
    pre_up = jnp.dot(inputs, w_up.T, preferred_element_type=jnp.float32) * in_scale
    hid_grad = jnp.dot(out_grad, w_down.T, preferred_element_type=jnp.float32) * hid_scale
    sigma = jax.nn.sigmoid(pre_gate)
    up_grad = (hid_grad * pre_gate * sigma).astype(jnp.bfloat16)
    gate_grad = (hid_grad * pre_up * sigma * (1.0 + pre_gate * (1.0 - sigma))).astype(jnp.bfloat16)
    weight_grad = jnp.dot(up_grad.T, inputs, preferred_element_type=jnp.float32) * in_scale
    input_grad = (jnp.dot(gate_grad, w_gate, preferred_element_type=jnp.float32) + jnp.dot(up_grad, w_up, preferred_element_type=jnp.float32)) * in_scale
    first = beta_one * moment_one.astype(jnp.float32) + (1.0 - beta_one) * weight_grad
    second = beta_two * moment_two.astype(jnp.float32) + (1.0 - beta_two) * weight_grad * weight_grad
    updated = w_master * (1.0 - inner_rate * decay_rate) - inner_rate * (first / bias_one) / (jnp.sqrt(second / bias_two) + adam_eps)
    return (input_grad.astype(jnp.bfloat16), updated, first.astype(jnp.bfloat16), second.astype(jnp.bfloat16))

def reference(tokens_in, cotangent, gate_weight, up_master, down_weight, up_first, up_second, snapshot, global_params, outer_momentum):
    grads_list = []
    ups_list = []
    firsts_list = []
    seconds_list = []
    total = jnp.zeros((D, D), jnp.float32)
    for replica in range(N_REP):
        lower = replica * TOK_REP
        result = replica_step(tokens_in[lower:lower + TOK_REP], cotangent[lower:lower + TOK_REP], gate_weight[replica], up_master[replica], down_weight[replica], up_first[replica], up_second[replica])
        grads_list.append(result[0])
        ups_list.append(result[1])
        firsts_list.append(result[2])
        seconds_list.append(result[3])
        total = total + snapshot[replica].astype(jnp.float32)
    delta = global_params - total / N_REP
    momentum_new = outer_mu * outer_momentum + delta
    global_new = global_params - outer_rate * (delta + outer_mu * momentum_new)
    return (jnp.concatenate(grads_list, axis=0), jnp.stack(ups_list), jnp.stack(firsts_list), jnp.stack(seconds_list), global_new, momentum_new)
```

```python
import math

import jax
import jax.numpy as jnp
from jax import lax
from jax.sharding import PartitionSpec as P

D = 4096
FFW = 7168
NZ, NY, NX = 8, 2, 4

beta_one = 0.9
beta_two = 0.95
inner_rate = 0.02
decay_rate = 0.1
adam_eps = 1e-08
bias_one = 0.9999734386011124
bias_two = 0.9940794707796659
outer_rate = 0.7
outer_mu = 0.9

f32 = jnp.float32
bf16 = jnp.bfloat16


def shift(value, dz=0, dy=0, dx=0):
    pairs = []
    for z in range(NZ):
        for y in range(NY):
            for x in range(NX):
                there = ((z + dz) % NZ * NY + (y + dy) % NY) * NX + (x + dx) % NX
                pairs.append(((z * NY + y) * NX + x, there))
    return lax.ppermute(value, "fsdp", pairs)


def gather_ring(own, axis):
    size = {"dz": NZ, "dx": NX}[axis]
    half = size // 2
    blocks = [None] * size
    blocks[0] = own
    ahead, behind = own, own
    for step in range(1, half):
        ahead = shift(ahead, **{axis: -1})
        behind = shift(behind, **{axis: 1})
        blocks[step] = ahead
        blocks[size - step] = behind
    rows = own.shape[0] // 2
    upper = shift(ahead[:rows], **{axis: -1})
    lower = shift(behind[rows:], **{axis: 1})
    blocks[half] = jnp.concatenate([upper, lower], 0)
    return blocks


def scatter_ring(chunks, axis):
    size = len(chunks)
    half = size // 2
    rows = chunks[0].shape[0] // 2
    right = shift(chunks[half][:rows], **{axis: 1})
    left = shift(chunks[half][rows:], **{axis: -1})
    for step in range(half - 1, 0, -1):
        mine_r, mine_l = chunks[step], chunks[size - step]
        if step == half - 1:
            tr = jnp.concatenate([right.astype(f32) + mine_r[:rows].astype(f32), mine_r[rows:].astype(f32)], 0)
            tl = jnp.concatenate([mine_l[:rows].astype(f32), left.astype(f32) + mine_l[rows:].astype(f32)], 0)
        else:
            tr = right.astype(f32) + mine_r.astype(f32)
            tl = left.astype(f32) + mine_l.astype(f32)
        right = shift(tr.astype(bf16), **{axis: 1})
        left = shift(tl.astype(bf16), **{axis: -1})
    return chunks[0].astype(f32) + right.astype(f32) + left.astype(f32)


def scatter_direct(chunks, axis):
    total = chunks[0].astype(f32)
    for k in range(1, len(chunks)):
        total = total + shift(chunks[k], **{axis: k}).astype(f32)
    return total


def by_rows(left, right):
    return lax.dot_general(left, right, (((1,), (1,)), ((), ())), preferred_element_type=f32)


def local(
    tokens_in, cotangent, gate_weight, up_master, down_weight, up_first, up_second, snapshot, global_params, outer_momentum
):
    in_scale = 1.0 / math.sqrt(D)
    hid_scale = 1.0 / math.sqrt(FFW)
    w_gate = gate_weight[0]
    w_master = up_master[0]
    w_down = down_weight[0]
    w_up = w_master.astype(bf16)
    units = w_gate.shape[0]

    gates = jnp.concatenate([w_gate, shift(w_gate, dy=1)], 0)
    downs = jnp.concatenate([w_down, shift(w_down, dy=1)], 0)
    ups = jnp.concatenate([w_up, shift(w_up, dy=1)], 0)

    x_first = [tokens_in] + [shift(tokens_in, dx=-k) for k in range(1, NX)]
    x_row = jnp.concatenate(x_first, 0)
    x_all = jnp.concatenate(gather_ring(x_row, "dz"), 0)
    g_col = jnp.concatenate(gather_ring(cotangent, "dz"), 0)
    g_blocks = gather_ring(g_col, "dx")

    rows = tokens_in.shape[0]
    hid = jnp.stack([by_rows(g, downs).reshape(NZ, rows, 2 * units) for g in g_blocks], 1)
    hid_grad = hid.reshape(NZ * NX * rows, 2 * units) * hid_scale
    pre_gate = by_rows(x_all, gates) * in_scale
    pre_up = by_rows(x_all, ups) * in_scale
    sigma = jax.nn.sigmoid(pre_gate)
    up_grad = (hid_grad * pre_gate * sigma).astype(bf16)
    gate_grad = (hid_grad * pre_up * sigma * (1.0 + pre_gate * (1.0 - sigma))).astype(bf16)

    def weight_of(grads):
        return lax.dot_general(grads, x_all, (((0,), (0,)), ((), ())), preferred_element_type=f32) * in_scale

    theirs = shift(weight_of(up_grad[:, units:]).astype(bf16), dy=1)

    d_in = (
        (jnp.dot(gate_grad, gates, preferred_element_type=f32) + jnp.dot(up_grad, ups, preferred_element_type=f32)) * in_scale
    ).astype(bf16)
    half = D // 2
    d_a = d_in[:, :half].reshape(NZ, NX * rows, half)
    a_row = scatter_ring([d_a[k] for k in range(NZ)], "dz").astype(bf16).reshape(NX, rows, half)
    part_a = scatter_direct([a_row[k] for k in range(NX)], "dx")
    d_b = d_in[:, half:].reshape(NZ, NX, rows, half)
    b_col = scatter_ring([d_b[:, k].reshape(NZ * rows, half) for k in range(NX)], "dx").astype(bf16).reshape(NZ, rows, half)
    part_b = scatter_direct([b_col[k] for k in range(NZ)], "dz")
    input_grad = jnp.concatenate([part_a, part_b], 1).astype(bf16)

    weight_grad = weight_of(up_grad[:, :units]) + theirs.astype(f32)
    first = beta_one * up_first[0].astype(f32) + (1.0 - beta_one) * weight_grad
    second = beta_two * up_second[0].astype(f32) + (1.0 - beta_two) * weight_grad * weight_grad
    updated = w_master * (1.0 - inner_rate * decay_rate) - inner_rate * (first / bias_one) / (
        jnp.sqrt(second / bias_two) + adam_eps
    )

    reps = 4
    columns = global_params.shape[1]
    me = lax.axis_index("rep")

    def cut(k):
        return lax.dynamic_slice_in_dim(snapshot[0], lax.rem(me + k, reps) * columns, columns, 1)

    summed = cut(0).astype(f32)
    for k in range(1, reps):
        summed = summed + lax.ppermute(cut(k), "rep", [(r, (r + k) % reps) for r in range(reps)]).astype(f32)
    delta = global_params - summed / reps
    momentum_new = outer_mu * outer_momentum + delta
    global_new = global_params - outer_rate * (delta + outer_mu * momentum_new)
    return (
        input_grad,
        updated[None],
        first.astype(bf16)[None],
        second.astype(bf16)[None],
        global_new,
        momentum_new,
    )


def solution(mesh):
    rows = P(("rep", "fsdp"), None)
    units = P("rep", "fsdp", None)
    outer = P("fsdp", "rep")
    in_specs = (rows, rows, units, units, units, units, units, units, outer, outer)
    out_specs = (rows, units, units, units, outer, outer)
    return jax.shard_map(local, mesh=mesh, in_specs=in_specs, out_specs=out_specs, check_vma=False)
```

```python
import math

import jax
import jax.numpy as jnp
from jax import lax
from jax.experimental import pallas as pl
from jax.experimental.pallas import tpu as pltpu
from jax.sharding import PartitionSpec as P

D = 4096
FFW = 7168
NZ, NY, NX = 8, 2, 4
HALF = D // 2

beta_one = 0.9
beta_two = 0.95
inner_rate = 0.02
decay_rate = 0.1
adam_eps = 1e-08
bias_one = 0.9999734386011124
bias_two = 0.9940794707796659
outer_rate = 0.7
outer_mu = 0.9
in_scale = 1.0 / math.sqrt(D)
hid_scale = 1.0 / math.sqrt(FFW)

f32 = jnp.float32
bf16 = jnp.bfloat16
VMEM = pl.BlockSpec(memory_space=pltpu.VMEM)


def shift(value, dz=0, dy=0, dx=0):
    pairs = []
    for z in range(NZ):
        for y in range(NY):
            for x in range(NX):
                there = ((z + dz) % NZ * NY + (y + dy) % NY) * NX + (x + dx) % NX
                pairs.append(((z * NY + y) * NX + x, there))
    return lax.ppermute(value, "fsdp", pairs)


def tie(values, *others):
    return lax.optimization_barrier((values, others))[0]


def stack_kernel(*refs):
    *parts, out = refs
    row = 0
    for part in parts:
        rows = part.shape[0]
        out[pl.ds(row, rows)] = part[...].astype(out.dtype)
        row += rows


def stack(parts):
    rows = sum(p.shape[0] for p in parts)
    return pl.pallas_call(
        stack_kernel,
        out_shape=jax.ShapeDtypeStruct((rows, parts[0].shape[1]), bf16),
        in_specs=[VMEM] * len(parts),
        out_specs=VMEM,
        compiler_params=pltpu.CompilerParams(vmem_limit_bytes=4 * 2**20),
        cost_estimate=pl.CostEstimate(flops=0, bytes_accessed=4 * rows * parts[0].shape[1], transcendentals=0),
        name="stack",
    )(*parts)


def nt(left, right):
    return lax.dot_general(left, right, (((1,), (1,)), ((), ())), preferred_element_type=f32)


def tn(left, right):
    return lax.dot_general(left, right, (((0,), (0,)), ((), ())), preferred_element_type=f32)


def x_rows(x_parts, half, at):
    parts = x_parts[:4] if half == 0 else x_parts[4:]
    return jnp.concatenate([part[:, at] for part in parts], 0)


def g_rows(g_parts, half, at):
    rows = []
    for z in range(4):
        for part, start in ((g_parts[0], 64 * half), (g_parts[1], 64 * half), (g_parts[2 + half], 0), (g_parts[4], 64 * half)):
            rows.append(part[pl.ds(start + 16 * z, 16), at])
    return jnp.concatenate(rows, 0)


def pair(weight, at):
    return jnp.concatenate([weight[0][:, at], weight[1][:, at]], 0)


def forward_kernel(*refs):
    x_parts, g_parts, gate, up, down = refs[:9], refs[9:14], refs[14:16], refs[16:18], refs[18:20]
    up_grad, gate_grad = refs[20:]
    width = 512
    slices = [pl.ds(c * width, width) for c in range(D // width)]
    for half in range(2):
        grad = pre_gate = pre_up = 0.0
        for at in slices:
            grad += nt(g_rows(g_parts, half, at), pair(down, at))
        for at in slices:
            part = x_rows(x_parts, half, at)
            pre_gate += nt(part, pair(gate, at))
            pre_up += nt(part, pair(up, at))
        grad, pre_gate, pre_up = grad * hid_scale, pre_gate * in_scale, pre_up * in_scale
        sigma = jax.nn.sigmoid(pre_gate)
        to = pl.ds(256 * half, 256)
        up_grad[to] = (grad * pre_gate * sigma).astype(bf16)
        gate_grad[to] = (grad * pre_up * sigma * (1.0 + pre_gate * (1.0 - sigma))).astype(bf16)


def forward(x_parts, g_parts, gate, up, down):
    tokens, units = 512, gate[0].shape[0]
    grads = jax.ShapeDtypeStruct((tokens, 2 * units), bf16)
    return pl.pallas_call(
        forward_kernel,
        out_shape=(grads, grads),
        in_specs=[VMEM] * 20,
        out_specs=(VMEM, VMEM),
        compiler_params=pltpu.CompilerParams(vmem_limit_bytes=16 * 2**20),
        cost_estimate=pl.CostEstimate(flops=6 * tokens * 2 * units * D, bytes_accessed=14 * 2**20, transcendentals=0),
        name="forward",
    )(*x_parts, *g_parts, *gate, *up, *down)


def input_kernel(*refs):
    up_grad, gate_grad, gate, up = refs[0], refs[1], refs[2:4], refs[4:6]
    a_parts, b_parts = refs[6:14], refs[14:]
    width = 512
    for c in range(D // width):
        at = pl.ds(c * width, width)
        out = jnp.dot(gate_grad[...], pair(gate, at), preferred_element_type=f32)
        out += jnp.dot(up_grad[...], pair(up, at), preferred_element_type=f32)
        out = (out * in_scale).astype(bf16)
        if c * width < HALF:
            row = 0
            for part in a_parts:
                rows = part.shape[0]
                part[:, at] = out[row : row + rows]
                row += rows
        else:
            to = pl.ds(c * width - HALF, width)
            for z in range(NZ):
                for x in range(NX):
                    b_parts[x][pl.ds(z * 16, 16), to] = out[(z * NX + x) * 16 : (z * NX + x + 1) * 16]


def input_terms(grads, gate, up):
    units = gate[0].shape[0]
    a_rows = (64,) * NZ
    b_rows = (128,) * NX
    outs = pl.pallas_call(
        input_kernel,
        out_shape=tuple(jax.ShapeDtypeStruct((r, HALF), bf16) for r in a_rows + b_rows),
        in_specs=[VMEM] * 6,
        out_specs=(VMEM,) * 12,
        compiler_params=pltpu.CompilerParams(vmem_limit_bytes=12 * 2**20),
        cost_estimate=pl.CostEstimate(flops=4 * 512 * 2 * units * D, bytes_accessed=8 * 2**20, transcendentals=0),
        name="input_terms",
    )(*grads, *gate, *up)
    return outs[:8], outs[8:]


def weight_kernel(*refs):
    x_parts, up_grad, mine, far = refs[:9], *refs[9:]
    units = mine.shape[0]
    width = 512
    for c in range(D // width):
        at = pl.ds(c * width, width)
        part = jnp.concatenate([x_rows(x_parts, 0, at), x_rows(x_parts, 1, at)], 0)
        out = tn(up_grad[...], part) * in_scale
        mine[:, at] = out[:units]
        far[:, at] = out[units:].astype(bf16)


def weight_terms(x_parts, up_grad):
    units = up_grad.shape[1] // 2
    return pl.pallas_call(
        weight_kernel,
        out_shape=(jax.ShapeDtypeStruct((units, D), f32), jax.ShapeDtypeStruct((units, D), bf16)),
        in_specs=[VMEM] * 10,
        out_specs=(VMEM, VMEM),
        compiler_params=pltpu.CompilerParams(vmem_limit_bytes=12 * 2**20),
        cost_estimate=pl.CostEstimate(flops=2 * 512 * 2 * units * D, bytes_accessed=8 * 2**20, transcendentals=0),
        name="weight_terms",
    )(*x_parts, up_grad)


def plus(arrived, own):
    return (arrived.astype(f32) + own.astype(f32)).astype(bf16)


def local(
    tokens_in, cotangent, gate_weight, up_master, down_weight, up_first, up_second, snapshot, global_params, outer_momentum
):
    w_master = up_master[0]
    w_gate, w_down = gate_weight[0], down_weight[0]
    w_up = w_master.astype(bf16)

    core, far = lax.rem(lax.axis_index("rep"), 2), lax.axis_index("rep") // 2
    columns = global_params.shape[1]

    def cut(which):
        return [
            lax.dynamic_slice_in_dim(snapshot[0], (2 * k + which) * columns, columns, 1) for k in range(2)
        ]

    over = lax.ppermute(jnp.concatenate(cut(1 - core), 0), "rep", [(0, 1), (1, 0), (2, 3), (3, 2)])
    kept = jnp.concatenate(cut(core), 0).astype(f32) + over.astype(f32)
    half = kept.shape[0] // 2
    kept, sent = jnp.where(far == 0, kept[:half], kept[half:]), jnp.where(far == 0, kept[half:], kept[:half]).astype(bf16)

    down_far = shift(w_down, dy=1)
    g_up1, g_dn1 = shift(cotangent, dz=-1), shift(cotangent, dz=1)
    x1, x2, x3 = (shift(tokens_in, dx=-k) for k in (1, 2, 3))
    g_up2, g_dn2 = shift(g_up1, dz=-1), shift(g_dn1, dz=1)
    g_up2t, g_dn2t = tie((g_up2, g_dn2), x1, x2, x3, sent)
    got = lax.ppermute(sent, "rep", [(0, 2), (1, 3), (2, 0), (3, 1)])
    summed = kept + got.astype(f32)
    g_up3, g_dn3 = shift(g_up2t, dz=-1), shift(g_dn2t, dz=1)
    x_row = stack([tokens_in, x1, x2, x3])
    g_up4 = shift(g_up3, dz=-1)
    x_rowt = tie(x_row, g_up3, g_dn3)
    z_up1, z_dn1 = shift(x_rowt, dz=-1), shift(x_rowt, dz=1)
    g_col = stack([cotangent, g_up1, g_up2, g_up3, g_up4, g_dn3, g_dn2, g_dn1])
    g_r1, g_l1 = shift(g_col, dx=-1), shift(g_col, dx=1)
    gate_far = shift(tie(w_gate, down_far, g_col), dy=1)
    z_up1t, z_dn1t = tie((z_up1, z_dn1), g_col, summed)
    z_up2, z_dn2 = shift(z_up1t, dz=-1), shift(z_dn1t, dz=1)
    g_r1t, g_l1t = tie((g_r1, g_l1), z_up2, z_dn2)
    g_r2, g_l2 = shift(g_r1t[:64], dx=-1), shift(g_l1t[64:], dx=1)
    z_up3, z_dn3 = shift(z_up2, dz=-1), shift(z_dn2, dz=1)
    up_far = shift(tie(w_up, gate_far, z_up2, z_dn2), dy=1)
    z_up4, z_dn4 = shift(z_up3[:32], dz=-1), shift(z_dn3[32:], dz=1)

    x_parts = (x_row, z_up1, z_up2, z_up3, z_up4, z_dn4, z_dn3, z_dn2, z_dn1)
    g_parts = (g_col, g_r1, g_r2, g_l2, g_l1)
    gate, up, down = (w_gate, gate_far), (w_up, up_far), (w_down, down_far)
    grads = forward(x_parts, g_parts, gate, up, down)
    a, b = input_terms(grads, gate, up)

    right, left = shift(a[4], dz=1), shift(a[5], dz=-1)
    b1, b2, b3 = (shift(b[k], dx=k) for k in range(1, NX))
    mine, theirs = weight_terms(x_parts, tie(grads[0], a[0]))
    theirs = shift(theirs, dy=1)
    right, left = plus(right, a[3]), plus(left, a[6])
    right, left = shift(right, dz=1), shift(left, dz=-1)
    right, left = plus(right, a[2]), plus(left, a[7])
    right, left = shift(right, dz=1), shift(left, dz=-1)
    b1, b2, b3 = tie((b1, b2, b3), right, left)
    b_sum = (b[0].astype(f32) + b1.astype(f32) + b2.astype(f32) + b3.astype(f32)).astype(bf16).reshape(NZ, 16, HALF)
    right = plus(right, a[1])
    odd = lax.rem(lax.axis_index("fsdp") // (NY * NX), 2)
    theirs_b = jnp.where(odd == 1, jnp.stack([b_sum[k] for k in (7, 1, 3, 5)]), jnp.stack([b_sum[k] for k in (1, 3, 5, 7)]))
    right, theirs_b = lax.optimization_barrier((right, theirs_b))
    right = shift(right, dz=1)
    swapped = lax.ppermute(
        theirs_b, "fsdp", [(i, i ^ (NY * NX)) for i in range(NZ * NY * NX)]
    )
    b_even = jnp.stack([b_sum[k] for k in (0, 2, 4, 6)])
    b_even = plus(swapped, b_even)
    b_got = [shift(b_even[k], dz=2 * k) for k in range(1, NZ // 2)]
    weight_grad = mine + theirs.astype(f32)
    first = beta_one * up_first[0].astype(f32) + (1.0 - beta_one) * weight_grad
    second = beta_two * up_second[0].astype(f32) + (1.0 - beta_two) * weight_grad * weight_grad
    updated = w_master * (1.0 - inner_rate * decay_rate) - inner_rate * (first / bias_one) / (
        jnp.sqrt(second / bias_two) + adam_eps
    )
    right = tie(right, updated)
    a_sum = (a[0].astype(f32) + right.astype(f32) + left.astype(f32)).astype(bf16).reshape(NX, 16, HALF)
    a_got = [shift(a_sum[k], dx=k) for k in range(1, NX)]
    b_got = tie(b_got, a_sum)
    total_a = a_sum[0].astype(f32)
    for got in a_got:
        total_a = total_a + got.astype(f32)
    total_b = b_even[0].astype(f32)
    for got in b_got:
        total_b = total_b + got.astype(f32)
    input_grad = jnp.concatenate([total_a, total_b], 1).astype(bf16)

    delta = global_params - summed / 4
    momentum_new = outer_mu * outer_momentum + delta
    global_new = global_params - outer_rate * (delta + outer_mu * momentum_new)
    return (
        input_grad,
        updated[None],
        first.astype(bf16)[None],
        second.astype(bf16)[None],
        global_new,
        momentum_new,
    )


def solution(mesh):
    rows = P(("rep", "fsdp"), None)
    units = P("rep", "fsdp", None)
    outer = P("fsdp", "rep")
    in_specs = (rows, rows, units, units, units, units, units, units, outer, outer)
    out_specs = (rows, units, units, units, outer, outer)
    return jax.shard_map(local, mesh=mesh, in_specs=in_specs, out_specs=out_specs, check_vma=False)
```

```python
import math

import jax
import jax.numpy as jnp
from jax import lax
from jax.experimental import pallas as pl
from jax.experimental.pallas import tpu as pltpu
from jax.sharding import PartitionSpec as P

D = 4096
FFW = 7168
NZ, NY, NX = 8, 2, 4
HALF = D // 2

beta_one = 0.9
beta_two = 0.95
inner_rate = 0.02
decay_rate = 0.1
adam_eps = 1e-08
bias_one = 0.9999734386011124
bias_two = 0.9940794707796659
outer_rate = 0.7
outer_mu = 0.9
in_scale = 1.0 / math.sqrt(D)
hid_scale = 1.0 / math.sqrt(FFW)

f32 = jnp.float32
bf16 = jnp.bfloat16
VMEM = pl.BlockSpec(memory_space=pltpu.VMEM)


def shift(value, dz=0, dy=0, dx=0):
    pairs = []
    for z in range(NZ):
        for y in range(NY):
            for x in range(NX):
                there = ((z + dz) % NZ * NY + (y + dy) % NY) * NX + (x + dx) % NX
                pairs.append(((z * NY + y) * NX + x, there))
    return lax.ppermute(value, "fsdp", pairs)


def tie(values, *others):
    return lax.optimization_barrier((values, others))[0]


def stack_kernel(*refs):
    *parts, out = refs
    row = 0
    for part in parts:
        rows = part.shape[0]
        out[pl.ds(row, rows)] = part[...].astype(out.dtype)
        row += rows


def stack(parts):
    rows = sum(p.shape[0] for p in parts)
    return pl.pallas_call(
        stack_kernel,
        out_shape=jax.ShapeDtypeStruct((rows, parts[0].shape[1]), bf16),
        in_specs=[VMEM] * len(parts),
        out_specs=VMEM,
        compiler_params=pltpu.CompilerParams(vmem_limit_bytes=4 * 2**20),
        cost_estimate=pl.CostEstimate(flops=0, bytes_accessed=4 * rows * parts[0].shape[1], transcendentals=0),
        name="stack",
    )(*parts)


def nt(left, right):
    return lax.dot_general(left, right, (((1,), (1,)), ((), ())), preferred_element_type=f32)


def tn(left, right):
    return lax.dot_general(left, right, (((0,), (0,)), ((), ())), preferred_element_type=f32)


def x_rows(x_parts, half, at):
    parts = x_parts[:4] if half == 0 else x_parts[4:]
    return jnp.concatenate([part[:, at] for part in parts], 0)


def g_rows(g_parts, half, at):
    rows = []
    for z in range(4):
        for part, start in ((g_parts[0], 64 * half), (g_parts[1], 64 * half), (g_parts[2 + half], 0), (g_parts[4], 64 * half)):
            rows.append(part[pl.ds(start + 16 * z, 16), at])
    return jnp.concatenate(rows, 0)


def pair(own, far, place, at):
    units = own.shape[0]
    return jnp.concatenate([own[:, at], far[pl.ds(place * units, units), at]], 0)


def forward_kernel(*refs):
    x_parts, g_parts = refs[:9], refs[9:14]
    gate, up, down, two_far, up_far, up_grad, gate_grad = refs[14:]
    width = 512
    slices = [pl.ds(c * width, width) for c in range(D // width)]
    for half in range(2):
        grad = pre_gate = pre_up = 0.0
        for at in slices:
            grad += nt(g_rows(g_parts, half, at), pair(down, two_far, 1, at))
        for at in slices:
            part = x_rows(x_parts, half, at)
            pre_gate += nt(part, pair(gate, two_far, 0, at))
            pre_up += nt(part, pair(up, up_far, 0, at))
        grad, pre_gate, pre_up = grad * hid_scale, pre_gate * in_scale, pre_up * in_scale
        sigma = jax.nn.sigmoid(pre_gate)
        to = pl.ds(256 * half, 256)
        up_grad[to] = (grad * pre_gate * sigma).astype(bf16)
        gate_grad[to] = (grad * pre_up * sigma * (1.0 + pre_gate * (1.0 - sigma))).astype(bf16)


def forward(x_parts, g_parts, weights):
    tokens, units = 512, weights[0].shape[0]
    grads = jax.ShapeDtypeStruct((tokens, 2 * units), bf16)
    return pl.pallas_call(
        forward_kernel,
        out_shape=(grads, grads),
        in_specs=[VMEM] * 19,
        out_specs=(VMEM, VMEM),
        compiler_params=pltpu.CompilerParams(vmem_limit_bytes=10 * 2**20),
        cost_estimate=pl.CostEstimate(flops=6 * tokens * 2 * units * D, bytes_accessed=14 * 2**20, transcendentals=0),
        name="forward",
    )(*x_parts, *g_parts, *weights)


def input_kernel(*refs):
    up_grad, gate_grad, gate, up, two_far, up_far = refs[:6]
    a_parts, b_parts = refs[6:14], refs[14:]
    width = 512
    for c in range(D // width):
        at = pl.ds(c * width, width)
        out = jnp.dot(gate_grad[...], pair(gate, two_far, 0, at), preferred_element_type=f32)
        out += jnp.dot(up_grad[...], pair(up, up_far, 0, at), preferred_element_type=f32)
        out = (out * in_scale).astype(bf16)
        if c * width < HALF:
            row = 0
            for part in a_parts:
                rows = part.shape[0]
                part[:, at] = out[row : row + rows]
                row += rows
        else:
            to = pl.ds(c * width - HALF, width)
            for z in range(NZ):
                for x in range(NX):
                    b_parts[x][pl.ds(z * 16, 16), to] = out[(z * NX + x) * 16 : (z * NX + x + 1) * 16]


def input_terms(grads, weights):
    units = weights[0].shape[0]
    a_rows = (64,) * NZ
    b_rows = (128,) * NX
    outs = pl.pallas_call(
        input_kernel,
        out_shape=tuple(jax.ShapeDtypeStruct((r, HALF), bf16) for r in a_rows + b_rows),
        in_specs=[VMEM] * 6,
        out_specs=(VMEM,) * 12,
        compiler_params=pltpu.CompilerParams(vmem_limit_bytes=10 * 2**20),
        cost_estimate=pl.CostEstimate(flops=4 * 512 * 2 * units * D, bytes_accessed=8 * 2**20, transcendentals=0),
        name="input_terms",
    )(*grads, *weights)
    return outs[:8], outs[8:]


def weight_kernel(*refs):
    x_parts, up_grad, mine, far = refs[:9], *refs[9:]
    units = mine.shape[0]
    width = 512
    for c in range(D // width):
        at = pl.ds(c * width, width)
        part = jnp.concatenate([x_rows(x_parts, 0, at), x_rows(x_parts, 1, at)], 0)
        out = tn(up_grad[...], part) * in_scale
        mine[:, at] = out[:units]
        far[:, at] = out[units:].astype(bf16)


def weight_terms(x_parts, up_grad):
    units = up_grad.shape[1] // 2
    return pl.pallas_call(
        weight_kernel,
        out_shape=(jax.ShapeDtypeStruct((units, D), f32), jax.ShapeDtypeStruct((units, D), bf16)),
        in_specs=[VMEM] * 10,
        out_specs=(VMEM, VMEM),
        compiler_params=pltpu.CompilerParams(vmem_limit_bytes=10 * 2**20),
        cost_estimate=pl.CostEstimate(flops=2 * 512 * 2 * units * D, bytes_accessed=8 * 2**20, transcendentals=0),
        name="weight_terms",
    )(*x_parts, up_grad)


def plus(arrived, own):
    return (arrived.astype(f32) + own.astype(f32)).astype(bf16)


def local(
    tokens_in, cotangent, gate_weight, up_master, down_weight, up_first, up_second, snapshot, global_params, outer_momentum
):
    w_master = up_master[0]
    w_gate, w_down = gate_weight[0], down_weight[0]
    w_up = w_master.astype(bf16)

    core, far = lax.rem(lax.axis_index("rep"), 2), lax.axis_index("rep") // 2
    columns = global_params.shape[1]

    def cut(which):
        return [
            lax.dynamic_slice_in_dim(snapshot[0], (2 * k + which) * columns, columns, 1) for k in range(2)
        ]

    over = lax.ppermute(jnp.concatenate(cut(1 - core), 0), "rep", [(0, 1), (1, 0), (2, 3), (3, 2)])
    kept = jnp.concatenate(cut(core), 0).astype(f32) + over.astype(f32)
    half = kept.shape[0] // 2
    kept, sent = jnp.where(far == 0, kept[:half], kept[half:]), jnp.where(far == 0, kept[half:], kept[:half]).astype(bf16)

    two = stack([w_gate, w_down])
    two_far = shift(tie(two, sent), dy=1)
    g_up1, g_dn1 = shift(cotangent, dz=-1), shift(cotangent, dz=1)
    x1, x2, x3 = (shift(tokens_in, dx=-k) for k in (1, 2, 3))
    g_up2, g_dn2 = shift(g_up1, dz=-1), shift(g_dn1, dz=1)
    g_up2t, g_dn2t = tie((g_up2, g_dn2), x1, x2, x3)
    g_up3, g_dn3 = shift(g_up2t, dz=-1), shift(g_dn2t, dz=1)
    x_row = stack([tokens_in, x1, x2, x3])
    g_up4 = shift(g_up3, dz=-1)
    x_rowt = tie(x_row, g_up3, g_dn3)
    z_up1, z_dn1 = shift(x_rowt, dz=-1), shift(x_rowt, dz=1)
    g_col = stack([cotangent, g_up1, g_up2, g_up3, g_up4, g_dn3, g_dn2, g_dn1])
    g_r1, g_l1 = shift(g_col, dx=-1), shift(g_col, dx=1)
    z_up1t, z_dn1t = tie((z_up1, z_dn1), g_col)
    z_up2, z_dn2 = shift(z_up1t, dz=-1), shift(z_dn1t, dz=1)
    got = lax.ppermute(tie(sent, two_far), "rep", [(0, 2), (1, 3), (2, 0), (3, 1)])
    summed = kept + tie(got, g_col).astype(f32)
    delta = global_params - summed / 4
    momentum_new = outer_mu * outer_momentum + delta
    global_new = global_params - outer_rate * (delta + outer_mu * momentum_new)
    g_r1t, g_l1t = tie((g_r1, g_l1), z_up2, z_dn2, global_new)
    g_r2, g_l2 = shift(g_r1t[:64], dx=-1), shift(g_l1t[64:], dx=1)
    z_up3, z_dn3 = shift(z_up2, dz=-1), shift(z_dn2, dz=1)
    up_far = shift(tie(w_up, two_far, z_up2, z_dn2), dy=1)
    z_up4, z_dn4 = shift(z_up3[:32], dz=-1), shift(z_dn3[32:], dz=1)

    x_parts = (x_row, z_up1, z_up2, z_up3, z_up4, z_dn4, z_dn3, z_dn2, z_dn1)
    g_parts = (g_col, g_r1, g_r2, g_l2, g_l1)
    grads = forward(x_parts, g_parts, (w_gate, w_up, w_down, two_far, up_far))
    mine, theirs = weight_terms(x_parts, grads[0])
    a, b = input_terms(tie(grads, theirs), (w_gate, w_up, two_far, up_far))
    theirs = shift(theirs, dy=1)

    right, left = shift(a[4], dz=1), shift(a[5], dz=-1)
    b1, b2, b3 = (shift(b[k], dx=k) for k in range(1, NX))
    right, left = plus(right, a[3]), plus(left, a[6])
    right, left = shift(right, dz=1), shift(left, dz=-1)
    right, left = plus(right, a[2]), plus(left, a[7])
    right, left = shift(right, dz=1), shift(left, dz=-1)
    b1, b2, b3 = tie((b1, b2, b3), right, left)
    b_sum = (b[0].astype(f32) + b1.astype(f32) + b2.astype(f32) + b3.astype(f32)).astype(bf16).reshape(NZ, 16, HALF)
    right = plus(right, a[1])
    odd = lax.rem(lax.axis_index("fsdp") // (NY * NX), 2)
    theirs_b = jnp.where(odd == 1, jnp.stack([b_sum[k] for k in (7, 1, 3, 5)]), jnp.stack([b_sum[k] for k in (1, 3, 5, 7)]))
    right = tie(right, b1, b2, b3)
    right = shift(right, dz=1)
    swapped = lax.ppermute(
        theirs_b, "fsdp", [(i, i ^ (NY * NX)) for i in range(NZ * NY * NX)]
    )
    b_even = jnp.stack([b_sum[k] for k in (0, 2, 4, 6)])
    b_even = plus(swapped, b_even)
    b_got = [shift(b_even[k], dz=2 * k) for k in range(1, NZ // 2)]
    weight_grad = mine + theirs.astype(f32)
    first = beta_one * up_first[0].astype(f32) + (1.0 - beta_one) * weight_grad
    second = beta_two * up_second[0].astype(f32) + (1.0 - beta_two) * weight_grad * weight_grad
    updated = w_master * (1.0 - inner_rate * decay_rate) - inner_rate * (first / bias_one) / (
        jnp.sqrt(second / bias_two) + adam_eps
    )
    right = tie(right, updated)
    a_sum = (a[0].astype(f32) + right.astype(f32) + left.astype(f32)).astype(bf16).reshape(NX, 16, HALF)
    a_got = [shift(a_sum[k], dx=k) for k in range(1, NX)]
    b_got = tie(b_got, a_sum)
    total_a = a_sum[0].astype(f32)
    for got in a_got:
        total_a = total_a + got.astype(f32)
    total_b = b_even[0].astype(f32)
    for got in b_got:
        total_b = total_b + got.astype(f32)
    input_grad = jnp.concatenate([total_a, total_b], 1).astype(bf16)

    return (
        input_grad,
        updated[None],
        first.astype(bf16)[None],
        second.astype(bf16)[None],
        global_new,
        momentum_new,
    )


def solution(mesh):
    rows = P(("rep", "fsdp"), None)
    units = P("rep", "fsdp", None)
    outer = P("fsdp", "rep")
    in_specs = (rows, rows, units, units, units, units, units, units, outer, outer)
    out_specs = (rows, units, units, units, outer, outer)
    return jax.shard_map(local, mesh=mesh, in_specs=in_specs, out_specs=out_specs, check_vma=False)
```

```python
import math

import jax
import jax.numpy as jnp
from jax import lax
from jax.experimental import pallas as pl
from jax.experimental.pallas import tpu as pltpu
from jax.sharding import PartitionSpec as P

D = 4096
FFW = 7168
NZ, NY, NX = 8, 2, 4
HALF = D // 2

beta_one = 0.9
beta_two = 0.95
inner_rate = 0.02
decay_rate = 0.1
adam_eps = 1e-08
bias_one = 0.9999734386011124
bias_two = 0.9940794707796659
outer_rate = 0.7
outer_mu = 0.9
in_scale = 1.0 / math.sqrt(D)
hid_scale = 1.0 / math.sqrt(FFW)

f32 = jnp.float32
bf16 = jnp.bfloat16
VMEM = pl.BlockSpec(memory_space=pltpu.VMEM)


def shift(value, dz=0, dy=0, dx=0):
    pairs = []
    for z in range(NZ):
        for y in range(NY):
            for x in range(NX):
                there = ((z + dz) % NZ * NY + (y + dy) % NY) * NX + (x + dx) % NX
                pairs.append(((z * NY + y) * NX + x, there))
    return lax.ppermute(value, "fsdp", pairs)


def tie(values, *others):
    return lax.optimization_barrier((values, others))[0]


def stack_kernel(*refs):
    *parts, out = refs
    row = 0
    for part in parts:
        rows = part.shape[0]
        out[pl.ds(row, rows)] = part[...].astype(out.dtype)
        row += rows


def stack(parts):
    rows = sum(p.shape[0] for p in parts)
    return pl.pallas_call(
        stack_kernel,
        out_shape=jax.ShapeDtypeStruct((rows, parts[0].shape[1]), bf16),
        in_specs=[VMEM] * len(parts),
        out_specs=VMEM,
        compiler_params=pltpu.CompilerParams(vmem_limit_bytes=4 * 2**20),
        cost_estimate=pl.CostEstimate(flops=0, bytes_accessed=4 * rows * parts[0].shape[1], transcendentals=0),
        name="stack",
    )(*parts)


def nt(left, right):
    return lax.dot_general(left, right, (((1,), (1,)), ((), ())), preferred_element_type=f32)


def tn(left, right):
    return lax.dot_general(left, right, (((0,), (0,)), ((), ())), preferred_element_type=f32)


def x_rows(x_parts, half, at):
    parts = x_parts[:4] if half == 0 else x_parts[4:]
    return jnp.concatenate([part[:, at] for part in parts], 0)


def g_rows(g_parts, half, at):
    rows = []
    for z in range(4):
        for part, start in ((g_parts[0], 64 * half), (g_parts[1], 64 * half), (g_parts[2 + half], 0), (g_parts[4], 64 * half)):
            rows.append(part[pl.ds(start + 16 * z, 16), at])
    return jnp.concatenate(rows, 0)


def pair(own, far, place, at):
    units = own.shape[0]
    return jnp.concatenate([own[:, at], far[pl.ds(place * units, units), at]], 0)


def forward_kernel(*refs):
    x_parts, g_parts = refs[:9], refs[9:14]
    gate, up, down, two_far, up_far, up_grad, gate_grad = refs[14:]
    width = 512
    slices = [pl.ds(c * width, width) for c in range(D // width)]
    for half in range(2):
        grad = pre_gate = pre_up = 0.0
        for at in slices:
            grad += nt(g_rows(g_parts, half, at), pair(down, two_far, 1, at))
        for at in slices:
            part = x_rows(x_parts, half, at)
            pre_gate += nt(part, pair(gate, two_far, 0, at))
            pre_up += nt(part, pair(up, up_far, 0, at))
        grad, pre_gate, pre_up = grad * hid_scale, pre_gate * in_scale, pre_up * in_scale
        sigma = jax.nn.sigmoid(pre_gate)
        to = pl.ds(256 * half, 256)
        up_grad[to] = (grad * pre_gate * sigma).astype(bf16)
        gate_grad[to] = (grad * pre_up * sigma * (1.0 + pre_gate * (1.0 - sigma))).astype(bf16)


def forward(x_parts, g_parts, weights):
    tokens, units = 512, weights[0].shape[0]
    grads = jax.ShapeDtypeStruct((tokens, 2 * units), bf16)
    return pl.pallas_call(
        forward_kernel,
        out_shape=(grads, grads),
        in_specs=[VMEM] * 19,
        out_specs=(VMEM, VMEM),
        compiler_params=pltpu.CompilerParams(vmem_limit_bytes=10 * 2**20),
        cost_estimate=pl.CostEstimate(flops=6 * tokens * 2 * units * D, bytes_accessed=14 * 2**20, transcendentals=0),
        name="forward",
    )(*x_parts, *g_parts, *weights)


def input_kernel(*refs):
    up_grad, gate_grad, gate, up, two_far, up_far = refs[:6]
    a_parts, b_parts = refs[6:14], refs[14:]
    width = 512
    for c in range(D // width):
        at = pl.ds(c * width, width)
        out = jnp.dot(gate_grad[...], pair(gate, two_far, 0, at), preferred_element_type=f32)
        out += jnp.dot(up_grad[...], pair(up, up_far, 0, at), preferred_element_type=f32)
        out = (out * in_scale).astype(bf16)
        if c * width < HALF:
            row = 0
            for part in a_parts:
                rows = part.shape[0]
                part[:, at] = out[row : row + rows]
                row += rows
        else:
            to = pl.ds(c * width - HALF, width)
            for z in range(NZ):
                for x in range(NX):
                    b_parts[x][pl.ds(z * 16, 16), to] = out[(z * NX + x) * 16 : (z * NX + x + 1) * 16]


def input_terms(grads, weights):
    units = weights[0].shape[0]
    a_rows = (64,) * NZ
    b_rows = (128,) * NX
    outs = pl.pallas_call(
        input_kernel,
        out_shape=tuple(jax.ShapeDtypeStruct((r, HALF), bf16) for r in a_rows + b_rows),
        in_specs=[VMEM] * 6,
        out_specs=(VMEM,) * 12,
        compiler_params=pltpu.CompilerParams(vmem_limit_bytes=10 * 2**20),
        cost_estimate=pl.CostEstimate(flops=4 * 512 * 2 * units * D, bytes_accessed=8 * 2**20, transcendentals=0),
        name="input_terms",
    )(*grads, *weights)
    return outs[:8], outs[8:]


def weight_kernel(*refs):
    x_parts, up_grad, mine, far = refs[:9], *refs[9:]
    units = mine.shape[0]
    width = 512
    for c in range(D // width):
        at = pl.ds(c * width, width)
        part = jnp.concatenate([x_rows(x_parts, 0, at), x_rows(x_parts, 1, at)], 0)
        out = tn(up_grad[...], part) * in_scale
        mine[:, at] = out[:units]
        far[:, at] = out[units:].astype(bf16)


def weight_terms(x_parts, up_grad):
    units = up_grad.shape[1] // 2
    return pl.pallas_call(
        weight_kernel,
        out_shape=(jax.ShapeDtypeStruct((units, D), f32), jax.ShapeDtypeStruct((units, D), bf16)),
        in_specs=[VMEM] * 10,
        out_specs=(VMEM, VMEM),
        compiler_params=pltpu.CompilerParams(vmem_limit_bytes=10 * 2**20),
        cost_estimate=pl.CostEstimate(flops=2 * 512 * 2 * units * D, bytes_accessed=8 * 2**20, transcendentals=0),
        name="weight_terms",
    )(*x_parts, up_grad)


def sum_kernel(*refs):
    *terms, out = refs
    total = terms[0][...].astype(f32)
    for term in terms[1:]:
        total += term[...].astype(f32)
    out[...] = total.astype(bf16)


def sum_of(terms):
    return pl.pallas_call(
        sum_kernel,
        out_shape=jax.ShapeDtypeStruct(terms[0].shape, bf16),
        in_specs=[VMEM] * len(terms),
        out_specs=VMEM,
        compiler_params=pltpu.CompilerParams(vmem_limit_bytes=4 * 2**20),
        cost_estimate=pl.CostEstimate(flops=0, bytes_accessed=terms[0].size, transcendentals=0),
        name="sum_of",
    )(*terms)


def plus(arrived, own):
    return (arrived.astype(f32) + own.astype(f32)).astype(bf16)


def local(
    tokens_in, cotangent, gate_weight, up_master, down_weight, up_first, up_second, snapshot, global_params, outer_momentum
):
    w_master = up_master[0]
    w_gate, w_down = gate_weight[0], down_weight[0]
    w_up = w_master.astype(bf16)

    core, far = lax.rem(lax.axis_index("rep"), 2), lax.axis_index("rep") // 2
    columns = global_params.shape[1]

    def cut(which):
        return [
            lax.dynamic_slice_in_dim(snapshot[0], (2 * k + which) * columns, columns, 1) for k in range(2)
        ]

    over = lax.ppermute(jnp.concatenate(cut(1 - core), 0), "rep", [(0, 1), (1, 0), (2, 3), (3, 2)])
    kept = jnp.concatenate(cut(core), 0).astype(f32) + over.astype(f32)
    half = kept.shape[0] // 2
    kept, sent = jnp.where(far == 0, kept[:half], kept[half:]), jnp.where(far == 0, kept[half:], kept[:half]).astype(bf16)

    two = stack([w_gate, w_down])
    two_far = shift(tie(two, sent), dy=1)
    g_up1, g_dn1 = shift(cotangent, dz=-1), shift(cotangent, dz=1)
    x1, x2, x3 = (shift(tokens_in, dx=-k) for k in (1, 2, 3))
    g_up2, g_dn2 = shift(g_up1, dz=-1), shift(g_dn1, dz=1)
    g_up2t, g_dn2t = tie((g_up2, g_dn2), x1, x2, x3)
    g_up3, g_dn3 = shift(g_up2t, dz=-1), shift(g_dn2t, dz=1)
    x_row = stack([tokens_in, x1, x2, x3])
    g_up4 = shift(g_up3, dz=-1)
    x_rowt = tie(x_row, g_up3, g_dn3)
    z_up1, z_dn1 = shift(x_rowt, dz=-1), shift(x_rowt, dz=1)
    g_col = stack([cotangent, g_up1, g_up2, g_up3, g_up4, g_dn3, g_dn2, g_dn1])
    g_r1, g_l1 = shift(g_col, dx=-1), shift(g_col, dx=1)
    z_up1t, z_dn1t = tie((z_up1, z_dn1), g_col)
    z_up2, z_dn2 = shift(z_up1t, dz=-1), shift(z_dn1t, dz=1)
    got = lax.ppermute(tie(sent, two_far), "rep", [(0, 2), (1, 3), (2, 0), (3, 1)])
    summed = kept + tie(got, g_col).astype(f32)
    delta = global_params - summed / 4
    momentum_new = outer_mu * outer_momentum + delta
    global_new = global_params - outer_rate * (delta + outer_mu * momentum_new)
    g_r1t, g_l1t = tie((g_r1, g_l1), z_up2, z_dn2, global_new)
    g_r2, g_l2 = shift(g_r1t[:64], dx=-1), shift(g_l1t[64:], dx=1)
    z_up3, z_dn3 = shift(z_up2, dz=-1), shift(z_dn2, dz=1)
    up_far = shift(tie(w_up, two_far, z_up2, z_dn2), dy=1)
    z_up4, z_dn4 = shift(z_up3[:32], dz=-1), shift(z_dn3[32:], dz=1)

    x_parts = (x_row, z_up1, z_up2, z_up3, z_up4, z_dn4, z_dn3, z_dn2, z_dn1)
    g_parts = (g_col, g_r1, g_r2, g_l2, g_l1)
    grads = forward(x_parts, g_parts, (w_gate, w_up, w_down, two_far, up_far))
    mine, theirs = weight_terms(x_parts, grads[0])
    a, b = input_terms(tie(grads, theirs), (w_gate, w_up, two_far, up_far))
    theirs = shift(theirs, dy=1)

    right, left = shift(a[4], dz=1), shift(a[5], dz=-1)
    b1, b2, b3 = (shift(b[k], dx=k) for k in range(1, NX))
    right, left = plus(right, a[3]), plus(left, a[6])
    right, left = shift(right, dz=1), shift(left, dz=-1)
    right, left = plus(right, a[2]), plus(left, a[7])
    right, left = shift(right, dz=1), shift(left, dz=-1)
    b1, b2, b3 = tie((b1, b2, b3), right, left)
    b_sum = sum_of([b[0], b1, b2, b3]).reshape(NZ, 16, HALF)
    right = plus(right, a[1])
    odd = lax.rem(lax.axis_index("fsdp") // (NY * NX), 2)
    theirs_b = jnp.where(odd == 1, jnp.stack([b_sum[k] for k in (7, 1, 3, 5)]), jnp.stack([b_sum[k] for k in (1, 3, 5, 7)]))
    right = tie(right, b1, b2, b3)
    right = shift(right, dz=1)
    swapped = lax.ppermute(
        theirs_b, "fsdp", [(i, i ^ (NY * NX)) for i in range(NZ * NY * NX)]
    )
    b_even = jnp.stack([b_sum[k] for k in (0, 2, 4, 6)])
    b_even = plus(swapped, b_even)
    b_got = [shift(b_even[k], dz=2 * k) for k in range(1, NZ // 2)]
    weight_grad = mine + theirs.astype(f32)
    first = beta_one * up_first[0].astype(f32) + (1.0 - beta_one) * weight_grad
    second = beta_two * up_second[0].astype(f32) + (1.0 - beta_two) * weight_grad * weight_grad
    updated = w_master * (1.0 - inner_rate * decay_rate) - inner_rate * (first / bias_one) / (
        jnp.sqrt(second / bias_two) + adam_eps
    )
    right = tie(right, updated)
    a_sum = (a[0].astype(f32) + right.astype(f32) + left.astype(f32)).astype(bf16).reshape(NX, 16, HALF)
    a_got = [shift(a_sum[k], dx=k) for k in range(1, NX)]
    b_got = tie(b_got, a_sum)
    total_a = a_sum[0].astype(f32)
    for got in a_got:
        total_a = total_a + got.astype(f32)
    total_b = b_even[0].astype(f32)
    for got in b_got:
        total_b = total_b + got.astype(f32)
    input_grad = jnp.concatenate([total_a, total_b], 1).astype(bf16)

    return (
        input_grad,
        updated[None],
        first.astype(bf16)[None],
        second.astype(bf16)[None],
        global_new,
        momentum_new,
    )


def solution(mesh):
    rows = P(("rep", "fsdp"), None)
    units = P("rep", "fsdp", None)
    outer = P("fsdp", "rep")
    in_specs = (rows, rows, units, units, units, units, units, units, outer, outer)
    out_specs = (rows, units, units, units, outer, outer)
    return jax.shard_map(local, mesh=mesh, in_specs=in_specs, out_specs=out_specs, check_vma=False)
```
